1024 devices in a mesh: group: 32 (over z, core), bal: 32 (over x, y).
Axes of the slice: x: 4, y: 8, z: 16, core: 2. Of those that a mesh axis runs over, the one named last changes fastest.
Arguments:
- query_rows: bfloat16 [2048, 128, 512], P(('group', 'bal')), may hold values from -6 to 6
- key_rows: bfloat16 [2048, 128, 512], P(('group', 'bal')), may hold values from -6 to 6
- value_rows: bfloat16 [2048, 128, 512], P(('group', 'bal')), may hold values from -6 to 6
- gate_rows: bfloat16 [2048, 128, 512], P(('group', 'bal')), may hold values from -6 to 6
- upstream: bfloat16 [2048, 128, 1024], P(('group', 'bal')), may hold values from -6 to 6
- lengths: int32 [2048], P('group'), may hold values from 0 to 128
- route_plan: int32 [1024], P('group'), may hold values from 0 to 31
- out_weight: bfloat16 [512, 1024], replicated, may hold values from -0.25 to 0.25
- prune_scores: float32 [512, 1024], P('bal', 'group'), may hold values from -6 to 6
Outputs:
- grad_query: bfloat16 [2048, 128, 512], P(('group', 'bal'))
- grad_key: bfloat16 [2048, 128, 512], P(('group', 'bal'))
- grad_value: bfloat16 [2048, 128, 512], P(('group', 'bal'))
- grad_gate: bfloat16 [2048, 128, 512], P(('group', 'bal'))
- weight_grad: float32 [512, 1024], P('bal', 'group')
- new_scores: float32 [512, 1024], P('bal', 'group')
The draws below stay inside these ranges and needn't reach their ends.
All inputs are finite; a program needn't handle non-finite values.
Results may differ from the reference program's by a relative error of at most 0.0059.
Values may be sent and summed in bfloat16 or wider, within the bound.
No kernel may reach another device: no remote copies, remote signals or barrier semaphores. Data moves between devices by JAX's collectives and lax.ppermute only.
A program may use at most 32 MiB of HBM per device.

```python
import math
import jax
import jax.numpy as jnp
import numpy as np
from jax import lax

D = 1024
HEAD = 128
WIN = 512
TILE = 128
SLOTS = 2
TILES_ALL = 2048
TOKENS = 262144
N_GROUP = 32
N_BAL = 32


def with_ends(drawn, stream_key, smallest, largest):
    spot = [jax.random.randint(jax.random.fold_in(stream_key, axis), (), 0, length) for axis, length in enumerate(drawn.shape)]
    main_axis = drawn.shape.index(max(drawn.shape))
    neighbour = spot[:main_axis] + [(spot[main_axis] + 1) % drawn.shape[main_axis]] + spot[main_axis + 1:]
    return drawn.at[tuple(spot)].set(smallest).at[tuple(neighbour)].set(largest)


def levels(own_key, dims, shards, smallest, high):
    factor_of, own = 1.0, jax.random.fold_in(own_key, 6)
    for axis_at, parts in shards:
        heights = jnp.exp(jax.random.uniform(jax.random.fold_in(own, axis_at), (parts,), jnp.float32, smallest / len(shards), high / len(shards)))
        factor_of = factor_of * jnp.repeat(heights, dims[axis_at] // parts).reshape([-1 if axis == axis_at else 1 for axis in range(len(dims))])
    return factor_of


def noise(own_key, extent, deviation, most, split=(), kind=jnp.bfloat16):
    values = deviation * jax.random.normal(own_key, extent, jnp.float32)
    if split:
        values = values * levels(own_key, extent, split, -0.22, 0.18)
    return jnp.clip(values, -most, most).astype(kind)


def setup_inputs(seed: int = 0) -> dict:
    arg_keys = jax.random.split(jax.random.key(seed), 10)
    return {
        "query_rows": noise(arg_keys[0], (TILES_ALL, TILE, WIN), 1.0, 6.0, ((0, 1024),)),
        "key_rows": noise(arg_keys[1], (TILES_ALL, TILE, WIN), 1.0, 6.0, ((0, 1024),)),
        "value_rows": noise(arg_keys[2], (TILES_ALL, TILE, WIN), 1.0, 6.0, ((0, 1024),)),
        "gate_rows": noise(arg_keys[3], (TILES_ALL, TILE, WIN), 1.0, 6.0, ((0, 1024),)),
        "upstream": noise(arg_keys[4], (TILES_ALL, TILE, D), 1.0, 6.0, ((0, 1024),)),
        "lengths": with_ends(jax.random.randint(arg_keys[5], (TILES_ALL,), 0, TILE + 1), jax.random.fold_in(arg_keys[5], 1), 0, TILE).astype(jnp.int32),
        "route_plan": with_ends(jax.random.randint(arg_keys[6], (N_GROUP * N_BAL,), 0, SLOTS ** 5), jax.random.fold_in(arg_keys[6], 1), 0, (SLOTS ** 5) - 1).astype(jnp.int32),
        "out_weight": noise(arg_keys[7], (WIN, D), WIN ** -0.5, 0.25),
        "prune_scores": noise(arg_keys[8], (WIN, D), 1.0, 6.0, ((0, 32), (1, 32)), jnp.float32),
    }


def route_arrays(arrays, plan_table):
    slot_ids = jnp.arange(SLOTS, dtype=jnp.int32)
    segment_count = N_BAL.bit_length() - 1
    routed = list(arrays)
    for exchange_bit_position in range(segment_count):
        partners = np.arange(N_BAL) ^ 1 << exchange_bit_position
        choose = plan_table // SLOTS ** exchange_bit_position % SLOTS
        chosen = slot_ids[None, None, :] == choose[:, :, None]
        result = []
        for array in routed:
            extra = (1,) * (array.ndim - 3)
            index = choose.reshape(choose.shape + (1,) + extra).astype(jnp.int32)
            departing_tiles = jnp.take_along_axis(array, index, axis=2)
            received_tiles = departing_tiles[:, partners]
            result.append(jnp.where(chosen.reshape(chosen.shape + extra), received_tiles, array))
        routed = result
    return routed

def tile_backward(query_rows, key_rows, value_rows, gate_rows, upstream, lengths, out_weight):
    slot_total_count, tile_len, feat_width = query_rows.shape
    head_count = feat_width // HEAD
    head_shape = (slot_total_count, tile_len, head_count, HEAD)
    score_scale = 1.0 / math.sqrt(HEAD)
    positions = jnp.arange(tile_len, dtype=jnp.int32)
    live_rows = positions[None, :] < lengths[:, None]
    causal = positions[:, None] >= positions[None, :]
    pair_mask = (causal[None] & live_rows[:, None, :] & live_rows[:, :, None]).astype(jnp.float32)[:, None]
    query_heads = query_rows.astype(jnp.float32).reshape(head_shape)
    key_heads = key_rows.astype(jnp.float32).reshape(head_shape)
    value_heads = value_rows.astype(jnp.float32).reshape(head_shape)
    logits = jnp.einsum('sihd,sjhd->shij', query_heads, key_heads) * score_scale
    logit_sig = jax.nn.sigmoid(logits)
    attention = (logits * logit_sig / tile_len * pair_mask).astype(jnp.bfloat16)
    mixed_rows = jnp.einsum('shij,sjhd->sihd', attention.astype(jnp.float32), value_heads).reshape(slot_total_count, tile_len, feat_width)
    row_mean = lax.optimization_barrier(jnp.mean(mixed_rows, axis=-1, keepdims=True))
    centred = mixed_rows - row_mean
    variance = lax.optimization_barrier(jnp.mean(centred * centred, axis=-1, keepdims=True))
    inv_std = lax.rsqrt(variance + 1e-05)
    normed = centred * inv_std
    gate_f = gate_rows.astype(jnp.float32)
    gated_rows = (normed * gate_f).astype(jnp.bfloat16)
    grad_gated = jnp.einsum('sie,we->siw', upstream.astype(jnp.float32), out_weight.astype(jnp.float32))
    grad_gated = grad_gated * live_rows[:, :, None].astype(jnp.float32)
    grad_gate = (grad_gated * normed).astype(jnp.bfloat16)
    grad_normed = grad_gated * gate_f
    grad_mixed = inv_std * (grad_normed - lax.optimization_barrier(jnp.mean(grad_normed, axis=-1, keepdims=True)) - normed * lax.optimization_barrier(jnp.mean(grad_normed * normed, axis=-1, keepdims=True)))
    grad_mixed = grad_mixed.astype(jnp.bfloat16).astype(jnp.float32).reshape(head_shape)
    grad_attention = jnp.einsum('sihd,sjhd->shij', grad_mixed, value_heads)
    grad_logits = (grad_attention * logit_sig * (1.0 + logits * (1.0 - logit_sig)) / tile_len * pair_mask).astype(jnp.bfloat16)
    grad_logits = grad_logits.astype(jnp.float32)
    grad_value = jnp.einsum('shij,sihd->sjhd', attention.astype(jnp.float32), grad_mixed)
    grad_query = jnp.einsum('shij,sjhd->sihd', grad_logits, key_heads) * score_scale
    grad_key = jnp.einsum('shij,sihd->sjhd', grad_logits, query_heads) * score_scale
    flat_shape = (slot_total_count, tile_len, feat_width)
    partial_value = jnp.einsum('siw,sie->we', gated_rows.astype(jnp.float32), upstream.astype(jnp.float32))
    return (grad_query.reshape(flat_shape).astype(jnp.bfloat16), grad_key.reshape(flat_shape).astype(jnp.bfloat16), grad_value.reshape(flat_shape).astype(jnp.bfloat16), grad_gate, partial_value)

def reference(query_rows, key_rows, value_rows, gate_rows, upstream, lengths, route_plan, out_weight, prune_scores):
    lead = (N_GROUP, N_BAL, SLOTS)
    arrays = [query_rows.reshape(lead + (TILE, WIN)), key_rows.reshape(lead + (TILE, WIN)), value_rows.reshape(lead + (TILE, WIN)), gate_rows.reshape(lead + (TILE, WIN)), upstream.reshape(lead + (TILE, D)), lengths.reshape(lead)]
    plan_table = route_plan.reshape(N_GROUP, N_BAL)
    routed = route_arrays(arrays, plan_table)
    blocks = tuple((array.reshape((N_GROUP * N_BAL, SLOTS) + array.shape[3:]) for array in routed))

    def step_fn(total, block):
        outcome = tile_backward(block[0], block[1], block[2], block[3], block[4], block[5], out_weight)
        return (total + outcome[4], outcome[:4])
    start = jnp.zeros((WIN, D), jnp.float32)
    total, grads = lax.scan(step_fn, start, blocks)
    flat = (TILES_ALL, TILE, WIN)
    weight_grad = total * (1.0 / math.sqrt(TOKENS))
    new_scores = prune_scores - out_weight.astype(jnp.float32) * weight_grad
    return (grads[0].reshape(flat), grads[1].reshape(flat), grads[2].reshape(flat), grads[3].reshape(flat), weight_grad, new_scores)
```

```python
import math

import jax
import jax.numpy as jnp
from jax import lax
from jax.experimental import pallas as pl
from jax.experimental.pallas import tpu as pltpu
from jax.sharding import PartitionSpec as P

HEAD = 128
STRIP = 16
SMALL = 16 * 2**20
BIG = 60 * 2**20


def dot(a, b, ca, cb):
    return lax.dot_general(a, b, (((ca,), (cb,)), ((), ())), preferred_element_type=jnp.float32)


def heads_of(width):
    return [slice(h * HEAD, (h + 1) * HEAD) for h in range(width // HEAD)]


def grad_kernel(len_ref, plan_ref, *refs):
    far, (pieces, keep_ref, send_ref, from_ref, block_ref), near = refs[:6], refs[6:11], refs[11:17]
    z_ref, sum_ref, sems = refs[17:]
    copies = [pltpu.make_async_copy(a, b, sems.at[i]) for i, (a, b) in enumerate(zip(far, near))]
    for copy in copies:
        copy.start()
    q, k, v, u, g, w = near
    count, slots = plan_ref.shape[0], q.shape[0]
    for i in range(count * slots):
        from_ref[i] = i
    for t in range(count.bit_length() - 1):
        for low in range(count):
            high = low | 1 << t
            if high != low:
                a = low * slots + ((plan_ref[low] >> t) & 1)
                b = high * slots + ((plan_ref[high] >> t) & 1)
                held, other = from_ref[a], from_ref[b]
                from_ref[a] = other
                from_ref[b] = held
    for copy in copies:
        copy.wait()
    pos, group = lax.axis_index("bal"), lax.axis_index("group")
    rows, width = q.shape[1:]
    strips, share = rows // STRIP, width // HEAD * STRIP
    scale = 1.0 / math.sqrt(HEAD)

    def put(which, tile, h, value):
        at = slice(tile * share + h * STRIP, tile * share + (h + 1) * STRIP)
        value = value.astype(jnp.bfloat16).reshape(strips, STRIP, HEAD)
        pieces[which * strips : (which + 1) * strips, at, :] = value

    row_ids = lax.broadcasted_iota(jnp.int32, (rows, rows), 0)
    col_ids = lax.broadcasted_iota(jnp.int32, (rows, rows), 1)
    for tile in range(slots):
        live = len_ref[pos * slots + tile]
        allowed = (col_ids <= row_ids) & (row_ids < live)
        logits, sigs, atts, mixed = [], [], [], []
        for at in heads_of(width):
            s = dot(q[tile, :, at], k[tile, :, at], 1, 1) * scale
            sig = jax.nn.sigmoid(s)
            a = jnp.where(allowed, s * sig * (1.0 / rows), 0.0).astype(jnp.bfloat16)
            logits.append(s)
            sigs.append(sig)
            atts.append(a)
            mixed.append(dot(a, v[tile, :, at], 1, 0))
        o = jnp.concatenate(mixed, axis=1)
        centred = o - jnp.mean(o, axis=-1, keepdims=True)
        inv_std = lax.rsqrt(jnp.mean(centred * centred, axis=-1, keepdims=True) + 1e-05)
        normed = centred * inv_std
        gate = u[tile].astype(jnp.float32)
        z_ref[tile] = (normed * gate).astype(jnp.bfloat16)
        row_live = lax.broadcasted_iota(jnp.int32, (rows, 1), 0) < live
        dz = jnp.where(row_live, dot(g[tile], w[...], 1, 1), 0.0)
        grad_gate = dz * normed
        dn = dz * gate
        do = inv_std * (
            dn
            - jnp.mean(dn, axis=-1, keepdims=True)
            - normed * jnp.mean(dn * normed, axis=-1, keepdims=True)
        )
        do = do.astype(jnp.bfloat16)
        for h, at in enumerate(heads_of(width)):
            put(0, tile, h, grad_gate[:, at])
            doh = do[:, at]
            put(1, tile, h, dot(atts[h], doh, 0, 0))
            da = dot(doh, v[tile, :, at], 1, 1)
            s, sig = logits[h], sigs[h]
            ds = jnp.where(allowed, da * sig * (1.0 + s * (1.0 - sig)) * (1.0 / rows), 0.0)
            ds = ds.astype(jnp.bfloat16)
            put(2, tile, h, dot(ds, k[tile, :, at], 1, 0) * scale)
            put(3, tile, h, dot(ds, q[tile, :, at], 0, 0) * scale)
    total = sum(dot(g[tile], z_ref[tile], 0, 0) for tile in range(slots))
    sum_ref[...] = total.reshape(sum_ref.shape)
    core = group & 1
    own, block = block_ref.shape
    for out, which in ((keep_ref, core), (send_ref, 1 - core)):
        half = sum_ref[:, which].reshape(width, width).T
        for c, at in enumerate(heads_of(width)):
            out[:, c * own : (c + 1) * own, :] = half[:, at].reshape(count, own, HEAD)
    wide = w.shape[1]
    pick = lax.broadcasted_iota(jnp.int32, (wide, block), 0) == (
        lax.broadcasted_iota(jnp.int32, (wide, block), 1) + group * block
    )
    lines = w[pl.ds(pl.multiple_of(pos * own, own), own), :]
    block_ref[...] = dot(lines, pick.astype(jnp.float32).astype(jnp.bfloat16), 1, 0)


def order_kernel(from_ref, strips_ref, out_ref, sum_ref):
    count, lines = out_ref.shape[:2]
    share = lines // 2
    for at in range(count):
        for slot in range(2):
            source = from_ref[at * 2 + slot]
            row = pl.multiple_of((source & 1) * share, share)
            out_ref[at, slot * share : (slot + 1) * share, :] = strips_ref[source >> 1, pl.ds(row, share), :]
    sum_ref[...] = jnp.sum(strips_ref[:, lines:, :].astype(jnp.float32), axis=0)


def place_kernel(factor, strips_ref, sums_ref, block_ref, prune_ref, *outs):
    slots, rows, width = outs[0].shape
    strips, share = rows // STRIP, width // HEAD * STRIP
    for which in range(4):
        for slot in range(slots):
            for h, at in enumerate(heads_of(width)):
                lines = slice(slot * share + h * STRIP, slot * share + (h + 1) * STRIP)
                got = strips_ref[which * strips : (which + 1) * strips, lines, :]
                outs[which][slot, :, at] = got.reshape(rows, HEAD)
    own, block = outs[4].shape
    first = (lax.axis_index("group") >> 1) * block
    lines = pl.ds(pl.multiple_of(first // HEAD * own, own), own)
    total = jnp.sum(sums_ref[:, lines, :], axis=0)
    total = pltpu.roll(total, (HEAD - first % HEAD) % HEAD, 1)
    weight_grad = total[:, :block] * factor
    outs[4][...] = weight_grad
    outs[5][...] = prune_ref[...] - block_ref[...] * weight_grad


def per_device(query, key, value, gate, upstream, lengths, plan, out_weight, prune_scores):
    bal_count, group_count = lax.axis_size("bal"), lax.axis_size("group")
    slots, rows, width = query.shape
    out_width = upstream.shape[2]
    strips, heads = rows // STRIP, width // HEAD
    chips, block = group_count // 2, out_width // group_count
    own, lines = width // bal_count, slots * heads * STRIP
    smem = pl.BlockSpec(memory_space=pltpu.SMEM)
    vmem = pl.BlockSpec(memory_space=pltpu.VMEM)
    hbm = pl.BlockSpec(memory_space=pltpu.HBM)
    far = (query, key, value, gate, upstream, out_weight)

    def shape(*dims, kind=jnp.float32):
        return jax.ShapeDtypeStruct(dims, kind)

    half = shape(bal_count, heads * own, HEAD)
    pieces, keep, send, sources, weight_block = pl.pallas_call(
        grad_kernel,
        out_shape=[
            shape(bal_count, lines + heads * own, HEAD, kind=jnp.bfloat16),
            half,
            half,
            shape(bal_count * slots, kind=jnp.int32),
            shape(own, block),
        ],
        in_specs=[smem] * 2 + [hbm] * 6,
        out_specs=[vmem] * 3 + [smem, vmem],
        scratch_shapes=[pltpu.VMEM(a.shape, a.dtype) for a in far]
        + [
            pltpu.VMEM((slots, rows, width), jnp.bfloat16),
            pltpu.VMEM((chips, 2, block, width), jnp.float32),
            pltpu.SemaphoreType.DMA((6,)),
        ],
        compiler_params=pltpu.CompilerParams(vmem_limit_bytes=BIG),
        cost_estimate=pl.CostEstimate(flops=800_000_000, bytes_accessed=8_000_000, transcendentals=131072),
        name="tile_grads",
    )(lengths, plan, *far)

    cores = [(i, i ^ 1) for i in range(group_count)]
    total = keep + lax.ppermute(send, "group", cores)
    pieces = lax.dynamic_update_slice(pieces, total.astype(pieces.dtype), (0, lines, 0))
    spread = lax.all_to_all(pieces, "bal", 0, 0, tiled=True)
    routed, part = pl.pallas_call(
        order_kernel,
        out_shape=[shape(bal_count, lines, HEAD, kind=jnp.bfloat16), shape(heads * own, HEAD)],
        in_specs=[smem, vmem],
        out_specs=[vmem, vmem],
        compiler_params=pltpu.CompilerParams(vmem_limit_bytes=SMALL),
        cost_estimate=pl.CostEstimate(flops=0, bytes_accessed=2_000_000, transcendentals=0),
        name="routed_order",
    )(sources, spread)

    home = lax.all_to_all(routed, "bal", 0, 0, tiled=True)
    along = [[2 * z + core for z in range(chips)] for core in range(2)]
    parts = lax.all_gather(part, "group", axis_index_groups=along)
    tokens_all = group_count * bal_count * slots * rows
    outs = pl.pallas_call(
        lambda *refs: place_kernel(1.0 / math.sqrt(tokens_all), *refs),
        out_shape=[shape(slots, rows, width, kind=jnp.bfloat16)] * 4 + [shape(own, block)] * 2,
        in_specs=[vmem] * 4,
        out_specs=[vmem] * 6,
        compiler_params=pltpu.CompilerParams(vmem_limit_bytes=SMALL),
        name="place_grads",
    )(home, parts, weight_block, prune_scores)
    return (outs[2], outs[3], outs[1], outs[0], outs[4], outs[5])


def solution(mesh):
    tiles = P(("group", "bal"), None, None)
    return jax.shard_map(
        per_device,
        mesh=mesh,
        in_specs=(tiles,) * 5 + (P("group"), P("group"), P(), P("bal", "group")),
        out_specs=(tiles,) * 4 + (P("bal", "group"),) * 2,
        check_vma=False,
    )
```

```python
import math

import jax
import jax.numpy as jnp
from jax import lax
from jax.experimental import pallas as pl
from jax.experimental.pallas import tpu as pltpu
from jax.sharding import PartitionSpec as P

HEAD = 128
STRIP = 16
SMALL = 16 * 2**20
BIG = 60 * 2**20


def dot(a, b, ca, cb):
    return lax.dot_general(a, b, (((ca,), (cb,)), ((), ())), preferred_element_type=jnp.float32)


def heads_of(width):
    return [slice(h * HEAD, (h + 1) * HEAD) for h in range(width // HEAD)]


def grad_kernel(len_ref, plan_ref, *refs):
    far, (pieces, keep_ref, send_ref, from_ref, block_ref), near = refs[:6], refs[6:11], refs[11:17]
    z_ref, sum_ref, sems = refs[17:]
    copies = [pltpu.make_async_copy(a, b, sems.at[i]) for i, (a, b) in enumerate(zip(far, near))]
    for copy in copies:
        copy.start()
    q, k, v, u, g, w = near
    count, slots = plan_ref.shape[0], q.shape[0]
    for i in range(count * slots):
        from_ref[i] = i
    for t in range(count.bit_length() - 1):
        for low in range(count):
            high = low | 1 << t
            if high != low:
                a = low * slots + ((plan_ref[low] >> t) & 1)
                b = high * slots + ((plan_ref[high] >> t) & 1)
                held, other = from_ref[a], from_ref[b]
                from_ref[a] = other
                from_ref[b] = held
    pos, group = lax.axis_index("bal"), lax.axis_index("group")
    rows, width = q.shape[1:]
    strips, share = rows // STRIP, width // HEAD * STRIP
    scale = 1.0 / math.sqrt(HEAD)

    def put(which, tile, h, value):
        at = slice(tile * share + h * STRIP, tile * share + (h + 1) * STRIP)
        value = value.astype(jnp.bfloat16).reshape(strips, STRIP, HEAD)
        pieces[which * strips : (which + 1) * strips, at, :] = value

    row_ids = lax.broadcasted_iota(jnp.int32, (rows, rows), 0)
    col_ids = lax.broadcasted_iota(jnp.int32, (rows, rows), 1)
    for tile in range(slots):
        live = len_ref[pos * slots + tile]
        allowed = (col_ids <= row_ids) & (row_ids < live)
        if tile == 0:
            for copy in copies[:3]:
                copy.wait()
        logits, sigs, atts, mixed = [], [], [], []
        for at in heads_of(width):
            s = dot(q[tile, :, at], k[tile, :, at], 1, 1) * scale
            sig = jax.nn.sigmoid(s)
            a = jnp.where(allowed, s * sig * (1.0 / rows), 0.0).astype(jnp.bfloat16)
            logits.append(s)
            sigs.append(sig)
            atts.append(a)
            mixed.append(dot(a, v[tile, :, at], 1, 0))
        o = jnp.concatenate(mixed, axis=1)
        centred = o - jnp.mean(o, axis=-1, keepdims=True)
        inv_std = lax.rsqrt(jnp.mean(centred * centred, axis=-1, keepdims=True) + 1e-05)
        normed = centred * inv_std
        if tile == 0:
            for copy in copies[3:]:
                copy.wait()
        gate = u[tile].astype(jnp.float32)
        z_ref[tile] = (normed * gate).astype(jnp.bfloat16)
        row_live = lax.broadcasted_iota(jnp.int32, (rows, 1), 0) < live
        dz = jnp.where(row_live, dot(g[tile], w[...], 1, 1), 0.0)
        grad_gate = dz * normed
        dn = dz * gate
        do = inv_std * (
            dn
            - jnp.mean(dn, axis=-1, keepdims=True)
            - normed * jnp.mean(dn * normed, axis=-1, keepdims=True)
        )
        do = do.astype(jnp.bfloat16)
        for h, at in enumerate(heads_of(width)):
            put(0, tile, h, grad_gate[:, at])
            doh = do[:, at]
            put(1, tile, h, dot(atts[h], doh, 0, 0))
            da = dot(doh, v[tile, :, at], 1, 1)
            s, sig = logits[h], sigs[h]
            ds = jnp.where(allowed, da * sig * (1.0 + s * (1.0 - sig)) * (1.0 / rows), 0.0)
            ds = ds.astype(jnp.bfloat16)
            put(2, tile, h, dot(ds, k[tile, :, at], 1, 0) * scale)
            put(3, tile, h, dot(ds, q[tile, :, at], 0, 0) * scale)
    total = sum(dot(g[tile], z_ref[tile], 0, 0) for tile in range(slots))
    sum_ref[...] = total.reshape(sum_ref.shape)
    core = group & 1
    own, block = block_ref.shape
    near_count = sum_ref.shape[0] * block // HEAD
    for out, which in ((keep_ref, core), (send_ref, 1 - core)):
        for c in range(near_count):
            picked = [sum_ref[f * near_count + c, which] for f in range(HEAD // block)]
            half = jnp.concatenate(picked, axis=0).T
            out[:, c * own : (c + 1) * own, :] = half.reshape(count, own, HEAD)
    wide = w.shape[1]
    pick = lax.broadcasted_iota(jnp.int32, (wide, block), 0) == (
        lax.broadcasted_iota(jnp.int32, (wide, block), 1) + group * block
    )
    lines = w[pl.ds(pl.multiple_of(pos * own, own), own), :]
    block_ref[...] = dot(lines, pick.astype(jnp.float32).astype(jnp.bfloat16), 1, 0)


def order_kernel(from_ref, strips_ref, out_ref, sum_ref):
    count, lines = out_ref.shape[:2]
    share = lines // 2
    for at in range(count):
        for slot in range(2):
            source = from_ref[at * 2 + slot]
            row = pl.multiple_of((source & 1) * share, share)
            out_ref[at, slot * share : (slot + 1) * share, :] = strips_ref[source >> 1, pl.ds(row, share), :]
    sum_ref[...] = jnp.sum(strips_ref[:, lines:, :].astype(jnp.float32), axis=0)


def place_kernel(factor, strips_ref, sums_ref, block_ref, prune_ref, *outs):
    slots, rows, width = outs[0].shape
    strips, share = rows // STRIP, width // HEAD * STRIP
    for which in range(4):
        for slot in range(slots):
            for h, at in enumerate(heads_of(width)):
                lines = slice(slot * share + h * STRIP, slot * share + (h + 1) * STRIP)
                got = strips_ref[which * strips : (which + 1) * strips, lines, :]
                outs[which][slot, :, at] = got.reshape(rows, HEAD)
    own, block = outs[4].shape
    first = (lax.axis_index("group") >> 1) // (width // HEAD) * block
    total = pltpu.roll(sums_ref[...], (HEAD - first) % HEAD, 1)
    weight_grad = total[:, :block] * factor
    outs[4][...] = weight_grad
    outs[5][...] = prune_ref[...] - block_ref[...] * weight_grad


def per_device(query, key, value, gate, upstream, lengths, plan, out_weight, prune_scores):
    bal_count, group_count = lax.axis_size("bal"), lax.axis_size("group")
    slots, rows, width = query.shape
    out_width = upstream.shape[2]
    strips, heads = rows // STRIP, width // HEAD
    chips, block = group_count // 2, out_width // group_count
    own, lines = width // bal_count, slots * heads * STRIP
    smem = pl.BlockSpec(memory_space=pltpu.SMEM)
    vmem = pl.BlockSpec(memory_space=pltpu.VMEM)
    hbm = pl.BlockSpec(memory_space=pltpu.HBM)
    far = (query, key, value, gate, upstream, out_weight)

    def shape(*dims, kind=jnp.float32):
        return jax.ShapeDtypeStruct(dims, kind)

    half = shape(bal_count, heads * own, HEAD)
    pieces, keep, send, sources, weight_block = pl.pallas_call(
        grad_kernel,
        out_shape=[
            shape(bal_count, lines + heads * own, HEAD, kind=jnp.bfloat16),
            half,
            half,
            shape(bal_count * slots, kind=jnp.int32),
            shape(own, block),
        ],
        in_specs=[smem] * 2 + [hbm] * 6,
        out_specs=[vmem] * 3 + [smem, vmem],
        scratch_shapes=[pltpu.VMEM(a.shape, a.dtype) for a in far]
        + [
            pltpu.VMEM((slots, rows, width), jnp.bfloat16),
            pltpu.VMEM((chips, 2, block, width), jnp.float32),
            pltpu.SemaphoreType.DMA((6,)),
        ],
        compiler_params=pltpu.CompilerParams(vmem_limit_bytes=BIG),
        cost_estimate=pl.CostEstimate(flops=800_000_000, bytes_accessed=8_000_000, transcendentals=131072),
        name="tile_grads",
    )(lengths, plan, *far)

    cores = [(i, i ^ 1) for i in range(group_count)]
    total = keep + lax.ppermute(send, "group", cores)
    pieces = lax.dynamic_update_slice(pieces, total.astype(pieces.dtype), (0, lines, 0))
    spread = lax.all_to_all(pieces, "bal", 0, 0, tiled=True)
    routed, part = pl.pallas_call(
        order_kernel,
        out_shape=[shape(bal_count, lines, HEAD, kind=jnp.bfloat16), shape(heads * own, HEAD)],
        in_specs=[smem, vmem],
        out_specs=[vmem, vmem],
        compiler_params=pltpu.CompilerParams(vmem_limit_bytes=SMALL),
        cost_estimate=pl.CostEstimate(flops=0, bytes_accessed=2_000_000, transcendentals=0),
        name="routed_order",
    )(sources, spread)

    home = lax.all_to_all(routed, "bal", 0, 0, tiled=True)
    near_by = [[2 * (f * heads + c) + core for c in range(heads)] for f in range(chips // heads) for core in range(2)]
    far_off = [[2 * (f * heads + c) + core for f in range(chips // heads)] for c in range(heads) for core in range(2)]
    parts = lax.all_gather(part, "group", axis_index_groups=near_by)
    near = (lax.axis_index("group") >> 1) % heads
    parts = jnp.sum(lax.dynamic_slice_in_dim(parts, near * own, own, 1), axis=0)
    parts = lax.psum(parts, "group", axis_index_groups=far_off)
    tokens_all = group_count * bal_count * slots * rows
    outs = pl.pallas_call(
        lambda *refs: place_kernel(1.0 / math.sqrt(tokens_all), *refs),
        out_shape=[shape(slots, rows, width, kind=jnp.bfloat16)] * 4 + [shape(own, block)] * 2,
        in_specs=[vmem] * 4,
        out_specs=[vmem] * 6,
        compiler_params=pltpu.CompilerParams(vmem_limit_bytes=SMALL),
        name="place_grads",
    )(home, parts, weight_block, prune_scores)
    return (outs[2], outs[3], outs[1], outs[0], outs[4], outs[5])


def solution(mesh):
    tiles = P(("group", "bal"), None, None)
    return jax.shard_map(
        per_device,
        mesh=mesh,
        in_specs=(tiles,) * 5 + (P("group"), P("group"), P(), P("bal", "group")),
        out_specs=(tiles,) * 4 + (P("bal", "group"),) * 2,
        check_vma=False,
    )
```

```python
import math

import jax
import jax.numpy as jnp
from jax import lax
from jax.experimental import pallas as pl
from jax.experimental.pallas import tpu as pltpu
from jax.sharding import PartitionSpec as P

HEAD = 128
STRIP = 16
SMALL = 16 * 2**20
BIG = 60 * 2**20


def dot(a, b, ca, cb):
    return lax.dot_general(a, b, (((ca,), (cb,)), ((), ())), preferred_element_type=jnp.float32)


def heads_of(width):
    return [slice(h * HEAD, (h + 1) * HEAD) for h in range(width // HEAD)]


def grad_kernel(len_ref, plan_ref, *refs):
    far, (pieces, keep_ref, send_ref, from_ref, block_ref), near = refs[:6], refs[6:11], refs[11:17]
    z_ref, sum_ref, sems = refs[17:]
    copies = [pltpu.make_async_copy(a, b, sems.at[i]) for i, (a, b) in enumerate(zip(far, near))]
    for copy in copies:
        copy.start()
    q, k, v, u, g, w = near
    count, slots = plan_ref.shape[0], q.shape[0]
    for i in range(count * slots):
        from_ref[i] = i
    for t in range(count.bit_length() - 1):
        for low in range(count):
            high = low | 1 << t
            if high != low:
                a = low * slots + ((plan_ref[low] >> t) & 1)
                b = high * slots + ((plan_ref[high] >> t) & 1)
                held, other = from_ref[a], from_ref[b]
                from_ref[a] = other
                from_ref[b] = held
    pos, group = lax.axis_index("bal"), lax.axis_index("group")
    rows, width = q.shape[1:]
    strips, share = rows // STRIP, width // HEAD * STRIP
    scale = 1.0 / math.sqrt(HEAD)

    def put(which, tile, h, value):
        at = slice(tile * share + h * STRIP, tile * share + (h + 1) * STRIP)
        value = value.astype(jnp.bfloat16).reshape(strips, STRIP, HEAD)
        pieces[which * strips : (which + 1) * strips, at, :] = value

    row_ids = lax.broadcasted_iota(jnp.int32, (rows, rows), 0)
    col_ids = lax.broadcasted_iota(jnp.int32, (rows, rows), 1)
    for tile in range(slots):
        live = len_ref[pos * slots + tile]
        allowed = (col_ids <= row_ids) & (row_ids < live)
        if tile == 0:
            for copy in copies[:3]:
                copy.wait()
        logits, sigs, atts, mixed = [], [], [], []
        for at in heads_of(width):
            s = dot(q[tile, :, at], k[tile, :, at], 1, 1) * scale
            sig = jax.nn.sigmoid(s)
            a = jnp.where(allowed, s * sig * (1.0 / rows), 0.0).astype(jnp.bfloat16)
            logits.append(s)
            sigs.append(sig)
            atts.append(a)
            mixed.append(dot(a, v[tile, :, at], 1, 0))
        o = jnp.concatenate(mixed, axis=1)
        centred = o - jnp.mean(o, axis=-1, keepdims=True)
        inv_std = lax.rsqrt(jnp.mean(centred * centred, axis=-1, keepdims=True) + 1e-05)
        normed = centred * inv_std
        if tile == 0:
            for copy in copies[3:]:
                copy.wait()
        gate = u[tile].astype(jnp.float32)
        z_ref[tile] = (normed * gate).astype(jnp.bfloat16)
        row_live = lax.broadcasted_iota(jnp.int32, (rows, 1), 0) < live
        dz = jnp.where(row_live, dot(g[tile], w[...], 1, 1), 0.0)
        grad_gate = dz * normed
        dn = dz * gate
        do = inv_std * (
            dn
            - jnp.mean(dn, axis=-1, keepdims=True)
            - normed * jnp.mean(dn * normed, axis=-1, keepdims=True)
        )
        do = do.astype(jnp.bfloat16)
        for h, at in enumerate(heads_of(width)):
            put(0, tile, h, grad_gate[:, at])
            doh = do[:, at]
            put(1, tile, h, dot(atts[h], doh, 0, 0))
            da = dot(doh, v[tile, :, at], 1, 1)
            s, sig = logits[h], sigs[h]
            ds = jnp.where(allowed, da * sig * (1.0 + s * (1.0 - sig)) * (1.0 / rows), 0.0)
            ds = ds.astype(jnp.bfloat16)
            put(2, tile, h, dot(ds, k[tile, :, at], 1, 0) * scale)
            put(3, tile, h, dot(ds, q[tile, :, at], 0, 0) * scale)
    total = sum(dot(g[tile], z_ref[tile], 0, 0) for tile in range(slots))
    sum_ref[...] = total.reshape(sum_ref.shape)
    core = group & 1
    own, block = block_ref.shape
    near_count = sum_ref.shape[0] * block // HEAD
    for out, which in ((keep_ref, core), (send_ref, 1 - core)):
        for c in range(near_count):
            picked = [sum_ref[f * near_count + c, which] for f in range(HEAD // block)]
            half = jnp.concatenate(picked, axis=0).T
            out[:, c * own : (c + 1) * own, :] = half.reshape(count, own, HEAD).astype(out.dtype)
    wide = w.shape[1]
    pick = lax.broadcasted_iota(jnp.int32, (wide, block), 0) == (
        lax.broadcasted_iota(jnp.int32, (wide, block), 1) + group * block
    )
    lines = w[pl.ds(pl.multiple_of(pos * own, own), own), :]
    block_ref[...] = dot(lines, pick.astype(jnp.float32).astype(jnp.bfloat16), 1, 0)


def order_kernel(from_ref, strips_ref, out_ref, sum_ref):
    count, lines = out_ref.shape[:2]
    share = lines // 2
    for at in range(count):
        for slot in range(2):
            source = from_ref[at * 2 + slot]
            row = pl.multiple_of((source & 1) * share, share)
            out_ref[at, slot * share : (slot + 1) * share, :] = strips_ref[source >> 1, pl.ds(row, share), :]
    sum_ref[...] = jnp.sum(strips_ref[:, lines:, :].astype(jnp.float32), axis=0)


def place_kernel(factor, strips_ref, sums_ref, block_ref, prune_ref, *outs):
    slots, rows, width = outs[0].shape
    strips, share = rows // STRIP, width // HEAD * STRIP
    for which in range(4):
        for slot in range(slots):
            for h, at in enumerate(heads_of(width)):
                lines = slice(slot * share + h * STRIP, slot * share + (h + 1) * STRIP)
                got = strips_ref[which * strips : (which + 1) * strips, lines, :]
                outs[which][slot, :, at] = got.reshape(rows, HEAD)
    own, block = outs[4].shape
    first = (lax.axis_index("group") >> 1) // (width // HEAD) * block
    total = pltpu.roll(sums_ref[...], (HEAD - first) % HEAD, 1)
    weight_grad = total[:, :block] * factor
    outs[4][...] = weight_grad
    outs[5][...] = prune_ref[...] - block_ref[...] * weight_grad


def per_device(query, key, value, gate, upstream, lengths, plan, out_weight, prune_scores):
    bal_count, group_count = lax.axis_size("bal"), lax.axis_size("group")
    slots, rows, width = query.shape
    out_width = upstream.shape[2]
    strips, heads = rows // STRIP, width // HEAD
    chips, block = group_count // 2, out_width // group_count
    own, lines = width // bal_count, slots * heads * STRIP
    smem = pl.BlockSpec(memory_space=pltpu.SMEM)
    vmem = pl.BlockSpec(memory_space=pltpu.VMEM)
    hbm = pl.BlockSpec(memory_space=pltpu.HBM)
    far = (query, key, value, gate, upstream, out_weight)

    def shape(*dims, kind=jnp.float32):
        return jax.ShapeDtypeStruct(dims, kind)

    pieces, keep, send, sources, weight_block = pl.pallas_call(
        grad_kernel,
        out_shape=[
            shape(bal_count, lines + heads * own, HEAD, kind=jnp.bfloat16),
            shape(bal_count, heads * own, HEAD),
            shape(bal_count, heads * own, HEAD, kind=jnp.bfloat16),
            shape(bal_count * slots, kind=jnp.int32),
            shape(own, block),
        ],
        in_specs=[smem] * 2 + [hbm] * 6,
        out_specs=[vmem] * 3 + [smem, vmem],
        scratch_shapes=[pltpu.VMEM(a.shape, a.dtype) for a in far]
        + [
            pltpu.VMEM((slots, rows, width), jnp.bfloat16),
            pltpu.VMEM((chips, 2, block, width), jnp.float32),
            pltpu.SemaphoreType.DMA((6,)),
        ],
        compiler_params=pltpu.CompilerParams(vmem_limit_bytes=BIG),
        cost_estimate=pl.CostEstimate(flops=800_000_000, bytes_accessed=8_000_000, transcendentals=131072),
        name="tile_grads",
    )(lengths, plan, *far)

    cores = [(i, i ^ 1) for i in range(group_count)]
    total = keep + lax.ppermute(send, "group", cores).astype(jnp.float32)
    pieces = lax.dynamic_update_slice(pieces, total.astype(pieces.dtype), (0, lines, 0))
    spread = lax.all_to_all(pieces, "bal", 0, 0, tiled=True)
    routed, part = pl.pallas_call(
        order_kernel,
        out_shape=[shape(bal_count, lines, HEAD, kind=jnp.bfloat16), shape(heads * own, HEAD)],
        in_specs=[smem, vmem],
        out_specs=[vmem, vmem],
        compiler_params=pltpu.CompilerParams(vmem_limit_bytes=SMALL),
        cost_estimate=pl.CostEstimate(flops=0, bytes_accessed=2_000_000, transcendentals=0),
        name="routed_order",
    )(sources, spread)

    home = lax.all_to_all(routed, "bal", 0, 0, tiled=True)
    near_by = [[2 * (f * heads + c) + core for c in range(heads)] for f in range(chips // heads) for core in range(2)]
    far_off = [[2 * (f * heads + c) + core for f in range(chips // heads)] for c in range(heads) for core in range(2)]
    parts = lax.all_gather(part, "group", axis_index_groups=near_by)
    near = (lax.axis_index("group") >> 1) % heads
    parts = jnp.sum(lax.dynamic_slice_in_dim(parts, near * own, own, 1), axis=0)
    parts = lax.psum(parts, "group", axis_index_groups=far_off)
    tokens_all = group_count * bal_count * slots * rows
    outs = pl.pallas_call(
        lambda *refs: place_kernel(1.0 / math.sqrt(tokens_all), *refs),
        out_shape=[shape(slots, rows, width, kind=jnp.bfloat16)] * 4 + [shape(own, block)] * 2,
        in_specs=[vmem] * 4,
        out_specs=[vmem] * 6,
        compiler_params=pltpu.CompilerParams(vmem_limit_bytes=SMALL),
        name="place_grads",
    )(home, parts, weight_block, prune_scores)
    return (outs[2], outs[3], outs[1], outs[0], outs[4], outs[5])


def solution(mesh):
    tiles = P(("group", "bal"), None, None)
    return jax.shard_map(
        per_device,
        mesh=mesh,
        in_specs=(tiles,) * 5 + (P("group"), P("group"), P(), P("bal", "group")),
        out_specs=(tiles,) * 4 + (P("bal", "group"),) * 2,
        check_vma=False,
    )
```

```python
import math

import jax
import jax.numpy as jnp
from jax import lax
from jax.experimental import pallas as pl
from jax.experimental.pallas import tpu as pltpu
from jax.sharding import PartitionSpec as P

HEAD = 128
STRIP = 16
SMALL = 16 * 2**20
BIG = 60 * 2**20


def dot(a, b, ca, cb):
    return lax.dot_general(a, b, (((ca,), (cb,)), ((), ())), preferred_element_type=jnp.float32)


def heads_of(width):
    return [slice(h * HEAD, (h + 1) * HEAD) for h in range(width // HEAD)]


def grad_kernel(len_ref, plan_ref, *refs):
    far, (pieces, keep_ref, send_ref, from_ref, block_ref), near = refs[:6], refs[6:11], refs[11:17]
    z_ref, sum_ref, sems = refs[17:]
    copies = [pltpu.make_async_copy(a, b, sems.at[i]) for i, (a, b) in enumerate(zip(far, near))]
    for copy in copies:
        copy.start()
    q, k, v, u, g, w = near
    count, slots = plan_ref.shape[0], q.shape[0]
    for i in range(count * slots):
        from_ref[i] = i
    for t in range(count.bit_length() - 1):
        for low in range(count):
            high = low | 1 << t
            if high != low:
                a = low * slots + ((plan_ref[low] >> t) & 1)
                b = high * slots + ((plan_ref[high] >> t) & 1)
                held, other = from_ref[a], from_ref[b]
                from_ref[a] = other
                from_ref[b] = held
    pos, group = lax.axis_index("bal"), lax.axis_index("group")
    rows, width = q.shape[1:]
    strips, share = rows // STRIP, width // HEAD * STRIP
    scale = 1.0 / math.sqrt(HEAD)

    def put(which, tile, h, value):
        at = slice(tile * share + h * STRIP, tile * share + (h + 1) * STRIP)
        value = value.astype(jnp.bfloat16).reshape(strips, STRIP, HEAD)
        pieces[which * strips : (which + 1) * strips, at, :] = value

    row_ids = lax.broadcasted_iota(jnp.int32, (rows, rows), 0)
    col_ids = lax.broadcasted_iota(jnp.int32, (rows, rows), 1)
    for tile in range(slots):
        live = len_ref[pos * slots + tile]
        allowed = (col_ids <= row_ids) & (row_ids < live)
        if tile == 0:
            for copy in copies[:3]:
                copy.wait()
        logits, sigs, atts, mixed = [], [], [], []
        for at in heads_of(width):
            s = dot(q[tile, :, at], k[tile, :, at], 1, 1) * scale
            sig = jax.nn.sigmoid(s)
            a = jnp.where(allowed, s * sig * (1.0 / rows), 0.0).astype(jnp.bfloat16)
            logits.append(s)
            sigs.append(sig)
            atts.append(a)
            mixed.append(dot(a, v[tile, :, at], 1, 0))
        o = jnp.concatenate(mixed, axis=1)
        centred = o - jnp.mean(o, axis=-1, keepdims=True)
        inv_std = lax.rsqrt(jnp.mean(centred * centred, axis=-1, keepdims=True) + 1e-05)
        normed = centred * inv_std
        if tile == 0:
            for copy in copies[3:]:
                copy.wait()
        gate = u[tile].astype(jnp.float32)
        z_ref[tile] = (normed * gate).astype(jnp.bfloat16)
        row_live = lax.broadcasted_iota(jnp.int32, (rows, 1), 0) < live
        dz = jnp.where(row_live, dot(g[tile], w[...], 1, 1), 0.0)
        grad_gate = dz * normed
        dn = dz * gate
        do = inv_std * (
            dn
            - jnp.mean(dn, axis=-1, keepdims=True)
            - normed * jnp.mean(dn * normed, axis=-1, keepdims=True)
        )
        do = do.astype(jnp.bfloat16)
        for h, at in enumerate(heads_of(width)):
            put(0, tile, h, grad_gate[:, at])
            doh = do[:, at]
            put(1, tile, h, dot(atts[h], doh, 0, 0))
            da = dot(doh, v[tile, :, at], 1, 1)
            s, sig = logits[h], sigs[h]
            ds = jnp.where(allowed, da * sig * (1.0 + s * (1.0 - sig)) * (1.0 / rows), 0.0)
            ds = ds.astype(jnp.bfloat16)
            put(2, tile, h, dot(ds, k[tile, :, at], 1, 0) * scale)
            put(3, tile, h, dot(ds, q[tile, :, at], 0, 0) * scale)
    total = sum(dot(g[tile], z_ref[tile], 0, 0) for tile in range(slots))
    sum_ref[...] = total.reshape(sum_ref.shape)
    core = group & 1
    own, block = block_ref.shape
    near_count = sum_ref.shape[0] * block // HEAD
    for out, which in ((keep_ref, core), (send_ref, 1 - core)):
        for c in range(near_count):
            picked = [sum_ref[f * near_count + c, which] for f in range(HEAD // block)]
            half = jnp.concatenate(picked, axis=0).T
            out[:, c * own : (c + 1) * own, :] = half.reshape(count, own, HEAD).astype(out.dtype)
    wide = w.shape[1]
    pick = lax.broadcasted_iota(jnp.int32, (wide, block), 0) == (
        lax.broadcasted_iota(jnp.int32, (wide, block), 1) + group * block
    )
    lines = w[pl.ds(pl.multiple_of(pos * own, own), own), :]
    block_ref[...] = dot(lines, pick.astype(jnp.float32).astype(jnp.bfloat16), 1, 0)


def order_kernel(from_ref, strips_ref, out_ref, sum_ref):
    count, lines = out_ref.shape[:2]
    share = lines // 2
    for at in range(count):
        for slot in range(2):
            source = from_ref[at * 2 + slot]
            row = pl.multiple_of((source & 1) * share, share)
            out_ref[at, slot * share : (slot + 1) * share, :] = strips_ref[source >> 1, pl.ds(row, share), :]
    sum_ref[...] = jnp.sum(strips_ref[:, lines:, :].astype(jnp.float32), axis=0)


def place_kernel(factor, strips_ref, sums_ref, block_ref, prune_ref, *outs):
    slots, rows, width = outs[0].shape
    strips, share = rows // STRIP, width // HEAD * STRIP
    for which in range(4):
        for slot in range(slots):
            for h, at in enumerate(heads_of(width)):
                lines = slice(slot * share + h * STRIP, slot * share + (h + 1) * STRIP)
                got = strips_ref[which * strips : (which + 1) * strips, lines, :]
                outs[which][slot, :, at] = got.reshape(rows, HEAD)
    own, block = outs[4].shape
    first = (lax.axis_index("group") >> 1) // (width // HEAD) * block
    total = pltpu.roll(sums_ref[...], (HEAD - first) % HEAD, 1)
    weight_grad = total[:, :block] * factor
    outs[4][...] = weight_grad
    outs[5][...] = prune_ref[...] - block_ref[...] * weight_grad


def per_device(query, key, value, gate, upstream, lengths, plan, out_weight, prune_scores):
    bal_count, group_count = lax.axis_size("bal"), lax.axis_size("group")
    slots, rows, width = query.shape
    out_width = upstream.shape[2]
    strips, heads = rows // STRIP, width // HEAD
    chips, block = group_count // 2, out_width // group_count
    own, lines = width // bal_count, slots * heads * STRIP
    smem = pl.BlockSpec(memory_space=pltpu.SMEM)
    vmem = pl.BlockSpec(memory_space=pltpu.VMEM)
    hbm = pl.BlockSpec(memory_space=pltpu.HBM)
    far = (query, key, value, gate, upstream, out_weight)

    def shape(*dims, kind=jnp.float32):
        return jax.ShapeDtypeStruct(dims, kind)

    pieces, keep, send, sources, weight_block = pl.pallas_call(
        grad_kernel,
        out_shape=[
            shape(bal_count, lines + heads * own, HEAD, kind=jnp.bfloat16),
            shape(bal_count, heads * own, HEAD),
            shape(bal_count, heads * own, HEAD, kind=jnp.bfloat16),
            shape(bal_count * slots, kind=jnp.int32),
            shape(own, block),
        ],
        in_specs=[smem] * 2 + [hbm] * 6,
        out_specs=[vmem] * 3 + [smem, vmem],
        scratch_shapes=[pltpu.VMEM(a.shape, a.dtype) for a in far]
        + [
            pltpu.VMEM((slots, rows, width), jnp.bfloat16),
            pltpu.VMEM((chips, 2, block, width), jnp.float32),
            pltpu.SemaphoreType.DMA((6,)),
        ],
        compiler_params=pltpu.CompilerParams(vmem_limit_bytes=BIG),
        cost_estimate=pl.CostEstimate(flops=800_000_000, bytes_accessed=8_000_000, transcendentals=131072),
        name="tile_grads",
    )(lengths, plan, *far)

    cores = [(i, i ^ 1) for i in range(group_count)]
    total = keep + lax.ppermute(send, "group", cores).astype(jnp.float32)
    pieces = lax.dynamic_update_slice(pieces, total.astype(pieces.dtype), (0, lines, 0))
    spread = lax.all_to_all(pieces, "bal", 0, 0, tiled=True)
    routed, part = pl.pallas_call(
        order_kernel,
        out_shape=[shape(bal_count, lines, HEAD, kind=jnp.bfloat16), shape(heads * own, HEAD)],
        in_specs=[smem, vmem],
        out_specs=[vmem, vmem],
        compiler_params=pltpu.CompilerParams(vmem_limit_bytes=SMALL),
        cost_estimate=pl.CostEstimate(flops=0, bytes_accessed=2_000_000, transcendentals=0),
        name="routed_order",
    )(sources, spread)

    home = lax.all_to_all(routed, "bal", 0, 0, tiled=True)
    near_by = [[2 * (f * heads + c) + core for c in range(heads)] for f in range(chips // heads) for core in range(2)]
    far_off = [[2 * (f * heads + c) + core for f in range(chips // heads)] for c in range(heads) for core in range(2)]
    parts = lax.all_gather(part.astype(jnp.bfloat16), "group", axis_index_groups=near_by)
    near = (lax.axis_index("group") >> 1) % heads
    parts = lax.dynamic_slice_in_dim(parts, near * own, own, 1).astype(jnp.float32)
    parts = jnp.sum(parts, axis=0)
    parts = lax.psum(parts, "group", axis_index_groups=far_off)
    tokens_all = group_count * bal_count * slots * rows
    outs = pl.pallas_call(
        lambda *refs: place_kernel(1.0 / math.sqrt(tokens_all), *refs),
        out_shape=[shape(slots, rows, width, kind=jnp.bfloat16)] * 4 + [shape(own, block)] * 2,
        in_specs=[vmem] * 4,
        out_specs=[vmem] * 6,
        compiler_params=pltpu.CompilerParams(vmem_limit_bytes=SMALL),
        name="place_grads",
    )(home, parts, weight_block, prune_scores)
    return (outs[2], outs[3], outs[1], outs[0], outs[4], outs[5])


def solution(mesh):
    tiles = P(("group", "bal"), None, None)
    return jax.shard_map(
        per_device,
        mesh=mesh,
        in_specs=(tiles,) * 5 + (P("group"), P("group"), P(), P("bal", "group")),
        out_specs=(tiles,) * 4 + (P("bal", "group"),) * 2,
        check_vma=False,
    )
```
